512 devices in a mesh: sec: 32 (over z_lo, x, core), ch: 16 (over z_hi, y).
Axes of the slice: x: 4, y: 4, z: 16 (z_hi: 4, z_lo: 4; z = z_hi * 4 + z_lo), core: 2. Of those that a mesh axis runs over, the one named last changes fastest.
Arguments:
- diag_blocks: float32 [32, 512, 512], P('sec', None, 'ch'), as said below
- lower_blocks: float32 [32, 512, 512], P('sec', None, 'ch'), as said below
- upper_blocks: float32 [32, 512, 512], P('sec', None, 'ch'), as said below
- sources: float32 [32, 512, 4096], P('sec', None, 'ch'), may hold values from -6 to 6
Outputs:
- reduced_diag: float32 [32, 512, 512], P('sec', None, 'ch')
- reduced_sources: float32 [32, 512, 4096], P('sec', None, 'ch')
The draws below stay inside these ranges and needn't reach their ends.
Inputs may be any that keep to these rules, and one draw needn't show every extreme that they name: `diag_blocks`: every block's diagonal entries lie between 4 and 8; every off-diagonal entry has magnitude at most 2.1 / sqrt(512). `lower_blocks`: every entry has magnitude below 3.7. `upper_blocks`: every entry has magnitude below 3.7.
All inputs are finite; a program needn't handle non-finite values.
Results may differ from the reference program's by a relative error of at most 0.0001.
Values sent between devices are 32-bit elements; how exact they have to be, the bound alone decides.
A program may use at most 64 MiB of HBM per device.

```python
import math
import jax
import jax.numpy as jnp
from jax import lax

M = 512
LEVELS = 3
SECTORS = 32
RHS = 4096


def diagonal_values(key):
    base_key = jax.random.fold_in(key, 101)
    return jnp.exp(jax.random.uniform(base_key, (SECTORS, M), jnp.float32, math.log(4.0), math.log(8.0)))


def coupling_block(ratio_key, diag_vals, off_vals):
    ratios = jax.random.uniform(ratio_key, (SECTORS, M), jnp.float32, 0.28, 0.46)
    eye_mat = jnp.eye(M, dtype=jnp.float32)
    return off_vals * (1.0 - eye_mat) + (ratios * diag_vals)[:, :, None] * eye_mat


def draw_diag_blocks(key, part):
    diag_vals = diagonal_values(key)
    key = jax.random.fold_in(key, 11)
    spread = 0.7 / math.sqrt(M)
    off_vals = jnp.clip(jax.random.normal(key, (SECTORS, M, M), jnp.float32), -3.0, 3.0) * spread
    eye_mat = jnp.eye(M, dtype=jnp.float32)
    return off_vals * (1.0 - eye_mat) + diag_vals[:, :, None] * eye_mat


def draw_lower_blocks(key, part):
    diag_vals = diagonal_values(key)
    key = jax.random.fold_in(key, 23)
    ratio_key, noise_key = jax.random.split(key)
    spread = 0.3 / math.sqrt(M)
    off_vals = jnp.clip(jax.random.normal(noise_key, (SECTORS, M, M), jnp.float32), -3.0, 3.0) * spread
    return coupling_block(ratio_key, diag_vals, off_vals)


def draw_upper_blocks(key, part):
    diag_vals = diagonal_values(key)
    key = jax.random.fold_in(key, 29)
    ratio_key, noise_key = jax.random.split(key)
    spread = 0.3 / math.sqrt(M)
    off_vals = jnp.clip(jax.random.normal(noise_key, (SECTORS, M, M), jnp.float32), -3.0, 3.0) * spread
    return coupling_block(ratio_key, diag_vals, off_vals)


def level_of(key, dims, shards, smallest, top_value):
    level, own = 1.0, jax.random.fold_in(key, 6)
    for dim, blocks in shards:
        steps = jnp.exp(jax.random.uniform(jax.random.fold_in(own, dim), (blocks,), jnp.float32, smallest / len(shards), top_value / len(shards)))
        level = level * jnp.repeat(steps, dims[dim] // blocks).reshape([-1 if axis == dim else 1 for axis in range(len(dims))])
    return level


def bell_draw(stream_key, extent, scale, most, cuts=(), held_as=jnp.bfloat16):
    result = scale * jax.random.normal(stream_key, extent, jnp.float32)
    if cuts:
        result = result * level_of(stream_key, extent, cuts, -0.22, 0.18)
    return jnp.clip(result, -most, most).astype(held_as)


def setup_inputs(seed: int = 0) -> dict:
    arg_keys = jax.random.split(jax.random.key(seed), 5)
    diag_blocks = draw_diag_blocks(jax.random.fold_in(arg_keys[4], 71), 0)
    lower_blocks = draw_lower_blocks(jax.random.fold_in(arg_keys[4], 71), 0)
    upper_blocks = draw_upper_blocks(jax.random.fold_in(arg_keys[4], 71), 0)
    sources = bell_draw(arg_keys[3], (SECTORS, M, RHS), 1.0, 6.0, ((0, 32), (2, 16)), jnp.float32)
    return dict(diag_blocks=diag_blocks, lower_blocks=lower_blocks, upper_blocks=upper_blocks, sources=sources)


def product(left, right):
    return jnp.einsum("sij,sjk->sik", left, right, precision=lax.Precision.HIGHEST, preferred_element_type=jnp.float32)


def first_inverse(center):
    diag_vals = jnp.diagonal(center, axis1=1, axis2=2)
    recip = 1.0 / diag_vals
    eye_mat = jnp.eye(center.shape[-1], dtype=jnp.float32)
    off_part = center - diag_vals[:, :, None] * eye_mat
    return recip[:, :, None] * eye_mat - recip[:, :, None] * off_part * recip[:, None, :]


def shift_down(values, stride):
    padding = jnp.zeros((stride,) + values.shape[1:], jnp.float32)
    return jnp.concatenate([padding, values[:-stride]], 0)


def shift_up(values, stride):
    padding = jnp.zeros((stride,) + values.shape[1:], jnp.float32)
    return jnp.concatenate([values[stride:], padding], 0)


def reference(diag_blocks, lower_blocks, upper_blocks, sources):
    center = diag_blocks
    down_link = lower_blocks
    up_link = upper_blocks
    source = sources
    for level_no in range(LEVELS):
        stride = 2 ** level_no
        seed_inv = first_inverse(center)
        inverse = 2.0 * seed_inv - product(seed_inv, product(center, seed_inv))
        down_sol = product(inverse, down_link)
        up_sol = product(inverse, up_link)
        source_sol = product(inverse, source)
        new_center = center - product(down_link, shift_down(up_sol, stride)) - product(up_link, shift_up(down_sol, stride))
        source = source - product(down_link, shift_down(source_sol, stride)) - product(up_link, shift_up(source_sol, stride))
        if level_no < LEVELS - 1:
            new_down = -product(down_link, shift_down(down_sol, stride))
            new_up = -product(up_link, shift_up(up_sol, stride))
            down_link = new_down
            up_link = new_up
        center = new_center
    return center, source
```

```python
import functools

import jax
import jax.numpy as jnp
from jax import lax
from jax.experimental import pallas as pl
from jax.experimental.pallas import tpu as pltpu
from jax.sharding import PartitionSpec as P

LEVELS = 3
MESH = pl.DeviceIdType.MESH
F32 = jnp.float32
BF16 = jnp.bfloat16


def split(x):
    hi = x.astype(BF16)
    return hi, (x - hi.astype(F32)).astype(BF16)


def dot(a, b):
    return jnp.dot(a, b, preferred_element_type=F32)


def product(left, hi, lo):
    left_hi, left_lo = split(left)
    return dot(left_hi, hi) + (dot(left_lo, hi) + dot(left_hi, lo))


def kernel(sectors, m, a_in, l_in, u_in, b_in, a_out, b_out,
           wa, wl, wu, zm, zb, rm_dn, rm_up, rb_dn, rb_up, rs, source,
           inv_hi, inv_lo, l_hi, l_lo, u_hi, u_lo, load_sem, ssem, rsem):
    sec = lax.axis_index("sec")
    ch = lax.axis_index("ch")
    z, y = ch // 4, ch % 4
    ins = (a_in, l_in, u_in)
    whole = (wa, wl, wu)

    loads = [pltpu.make_async_copy(ins[i], whole[i].at[0, z, y], load_sem.at[i]) for i in range(3)]
    loads.append(pltpu.make_async_copy(b_in, rs, load_sem.at[3]))
    for load in loads:
        load.start()

    def zat(d):
        return (z + d) % 4

    def yat(d):
        return (y + d) % 4

    z_next, z_prev = (sec, zat(1) * 4 + y), (sec, zat(3) * 4 + y)
    y_next, y_prev, y_far = (sec, z * 4 + yat(1)), (sec, z * 4 + yat(3)), (sec, z * 4 + yat(2))
    strides = [2 ** k for k in range(LEVELS)]
    below = [sec - s >= 0 for s in strides]
    above = [sec + s < sectors for s in strides]

    barrier = pltpu.get_barrier_semaphore()
    for device in (z_next, z_prev, y_next, y_prev, y_far):
        pl.semaphore_signal(barrier, inc=1, device_id=device, device_id_type=MESH)
    for k, s in enumerate(strides):
        @pl.when(below[k])
        def _():
            pl.semaphore_signal(barrier, inc=1, device_id=(sec - s, ch), device_id_type=MESH)

        @pl.when(above[k])
        def _():
            pl.semaphore_signal(barrier, inc=1, device_id=(sec + s, ch), device_id_type=MESH)

    for k in range(LEVELS):
        @pl.when(jnp.logical_not(below[k]))
        def _():
            rm_dn[k] = jnp.zeros_like(rm_dn[k])
            rb_dn[k] = jnp.zeros_like(rb_dn[k])

        @pl.when(jnp.logical_not(above[k]))
        def _():
            rm_up[k] = jnp.zeros_like(rm_up[k])
            rb_up[k] = jnp.zeros_like(rb_up[k])

    for load in loads:
        load.wait()
    source[...] = rs[...].T

    peers = 5
    for k in range(LEVELS):
        peers = peers + below[k].astype(jnp.int32) + above[k].astype(jnp.int32)
    pl.semaphore_wait(barrier, peers)

    sent = []

    def copy(src, dst, index, device):
        return pltpu.make_async_remote_copy(
            src_ref=src, dst_ref=dst, send_sem=ssem.at[index], recv_sem=rsem.at[index],
            device_id=device, device_id_type=MESH)

    def push(ref, index, device):
        out = copy(ref, ref, index, device)
        out.start()
        sent.append(out)

    def arrived(ref, index):
        copy(ref, ref, index, y_next).wait_recv()

    def slab(i, dz, dy):
        return whole[i].at[0, zat(dz), yat(dy)]

    def half(i, dz, part):
        return whole[i].at[0, zat(dz), y, pl.ds(16 * part, 16)]

    def z_own(i):
        push(slab(i, 0, 0), 16 * i, z_next)
        push(slab(i, 0, 0), 16 * i + 1, z_prev)

    def y_send(i, r):
        push(slab(i, r, 0), 16 * i + 4 + r, y_next)
        push(slab(i, r, 0), 16 * i + 8 + r, y_prev)

    def z_relay(i):
        arrived(slab(i, 3, 0), 16 * i)
        push(half(i, 3, 0), 16 * i + 2, z_next)
        arrived(slab(i, 1, 0), 16 * i + 1)
        push(half(i, 1, 1), 16 * i + 3, z_prev)
        y_send(i, 3)
        y_send(i, 1)

    def z_last(i):
        arrived(half(i, 2, 0), 16 * i + 2)
        arrived(half(i, 2, 1), 16 * i + 3)
        y_send(i, 2)

    def y_relay(i, r):
        arrived(slab(i, r, 3), 16 * i + 4 + r)
        if r % 2 == 0:
            push(slab(i, r, 3), 16 * i + 12 + r, y_next)
        arrived(slab(i, r, 1), 16 * i + 8 + r)
        if r % 2 == 1:
            push(slab(i, r, 1), 16 * i + 12 + r, y_prev)

    def y_last(i):
        for r in range(4):
            arrived(slab(i, r, 2), 16 * i + 12 + r)

    z_own(0)
    z_own(1)
    y_send(0, 0)
    y_send(1, 0)
    y_send(2, 0)
    z_relay(0)
    z_own(2)
    y_relay(0, 0)
    y_relay(1, 0)
    y_relay(2, 0)
    y_relay(0, 1)
    y_relay(0, 3)
    z_relay(1)
    z_last(0)
    y_relay(1, 1)
    y_relay(1, 3)
    y_relay(0, 2)
    z_relay(2)
    z_last(1)
    y_relay(2, 1)
    y_relay(2, 3)

    def invert(k):
        block = wa[k].reshape(m, m)
        rows = lax.broadcasted_iota(jnp.int32, (m, m), 0)
        cols = lax.broadcasted_iota(jnp.int32, (m, m), 1)
        on = rows == cols
        diag = jnp.where(on, block, 0.0)
        across = 1.0 / jnp.sum(diag, axis=0, keepdims=True)
        down = 1.0 / jnp.sum(diag, axis=1, keepdims=True)
        start = jnp.where(on, across, -(down * block * across))
        block_hi, block_lo = split(block)
        start_hi, start_lo = split(start)
        inner = product(start, block_hi, block_lo)
        inverse = 2.0 * start - product(inner, start_hi, start_lo)
        inv_hi[...], inv_lo[...] = split(inverse)

    def y_arrived(i, k):
        base = 48 + 9 * (k - 1) + 3 * i
        arrived(whole[i].at[k, :, yat(3)], base)
        arrived(whole[i].at[k, :, yat(1)], base + 1)
        arrived(whole[i].at[k, :, yat(2)], base + 2)

    def y_push(i, k):
        base = 48 + 9 * (k - 1) + 3 * i
        push(whole[i].at[k, :, y], base, y_next)
        push(whole[i].at[k, :, y], base + 1, y_prev)
        push(whole[i].at[k, :, y], base + 2, y_far)

    shifts = []

    def shift(k, src_up, dst_up, src_dn, dst_dn, index):
        up = copy(src_up, dst_up, index, (sec + strides[k], ch))
        dn = copy(src_dn, dst_dn, index + 1, (sec - strides[k], ch))

        @pl.when(above[k])
        def _():
            up.start()

        @pl.when(below[k])
        def _():
            dn.start()

        shifts.append((k, up, dn))

    def shifted(k, dst_up, dst_dn, index):
        @pl.when(below[k])
        def _():
            arrived(dst_up, index)

        @pl.when(above[k])
        def _():
            arrived(dst_dn, index + 1)

    def update_source(k):
        shifted(k, rb_dn.at[k], rb_up.at[k], 66 + 4 * k + 2)
        source[...] = source[...] - product(rb_dn[k], l_hi[...], l_lo[...]) - product(rb_up[k], u_hi[...], u_lo[...])

    quarter = m // 4
    for k in range(LEVELS):
        index = 66 + 4 * k
        if k == 0:
            y_last(0)
        else:
            y_arrived(0, k)
        invert(k)
        if k == 0:
            y_relay(1, 2)
            z_last(2)
            y_relay(2, 2)
        if k == LEVELS - 1:
            zm[k, 0:32] = product(wl[k, z, y], inv_hi[...], inv_lo[...])
            zm[k, 32:64] = product(wu[k, z, y], inv_hi[...], inv_lo[...])
            shift(k, zm.at[k, pl.ds(32, 32)], rm_dn.at[k, pl.ds(32, 32)],
                  zm.at[k, pl.ds(0, 32)], rm_up.at[k, pl.ds(0, 32)], index)
        else:
            zm[k, 0:quarter] = product(wl[k, :, y].reshape(quarter, m), inv_hi[...], inv_lo[...])
            zm[k, quarter:] = product(wu[k, :, y].reshape(quarter, m), inv_hi[...], inv_lo[...])
            shift(k, zm.at[k], rm_dn.at[k], zm.at[k], rm_up.at[k], index)
        if k > 0:
            update_source(k - 1)
        zb[k] = product(source[...], inv_hi[...], inv_lo[...])
        shift(k, zb.at[k], rb_dn.at[k], zb.at[k], rb_up.at[k], index + 2)
        if k == 0:
            y_last(1)
            y_last(2)
        else:
            y_arrived(1, k)
            y_arrived(2, k)
        l_hi[...], l_lo[...] = split(wl[k].reshape(m, m))
        u_hi[...], u_lo[...] = split(wu[k].reshape(m, m))
        if k == LEVELS - 1:
            shifted(k, rm_dn.at[k, pl.ds(32, 32)], rm_up.at[k, pl.ds(0, 32)], index)
            a_out[...] = (wa[k, z, y] - product(rm_dn[k, 32:64], l_hi[...], l_lo[...])
                          - product(rm_up[k, 0:32], u_hi[...], u_lo[...]))
        else:
            shifted(k, rm_dn.at[k], rm_up.at[k], index)
            from_dn = product(rm_dn[k], l_hi[...], l_lo[...])
            from_up = product(rm_up[k], u_hi[...], u_lo[...])
            center = wa[k, :, y].reshape(quarter, m) - from_dn[quarter:] - from_up[:quarter]
            wa[k + 1, :, y] = center.reshape(4, quarter // 4, m)
            y_push(0, k + 1)
            wl[k + 1, :, y] = (-from_dn[:quarter]).reshape(4, quarter // 4, m)
            y_push(1, k + 1)
            wu[k + 1, :, y] = (-from_up[quarter:]).reshape(4, quarter // 4, m)
            y_push(2, k + 1)
    update_source(LEVELS - 1)
    b_out[...] = source[...].T

    for out in sent:
        out.wait_send()
    for k, up, dn in shifts:
        @pl.when(above[k])
        def _():
            up.wait_send()

        @pl.when(below[k])
        def _():
            dn.wait_send()


def shards(sectors, diag_blocks, lower_blocks, upper_blocks, sources):
    m = diag_blocks.shape[1]
    width = diag_blocks.shape[2]
    columns = sources.shape[2]
    quarter = m // 4
    copies = 66 + 4 * LEVELS
    vmem = pl.BlockSpec(memory_space=pltpu.VMEM)
    hbm = pl.BlockSpec(memory_space=pl.ANY)
    center, source = pl.pallas_call(
        functools.partial(kernel, sectors, m),
        out_shape=(jax.ShapeDtypeStruct((width, m), F32), jax.ShapeDtypeStruct((m, columns), F32)),
        in_specs=[hbm] * 4,
        out_specs=(vmem, vmem),
        scratch_shapes=[
            pltpu.VMEM((LEVELS, 4, 4, width, m), F32),
            pltpu.VMEM((LEVELS, 4, 4, width, m), F32),
            pltpu.VMEM((LEVELS, 4, 4, width, m), F32),
            pltpu.VMEM((LEVELS, 2 * quarter, m), F32),
            pltpu.VMEM((LEVELS, columns, m), F32),
            pltpu.VMEM((LEVELS, 2 * quarter, m), F32),
            pltpu.VMEM((LEVELS, 2 * quarter, m), F32),
            pltpu.VMEM((LEVELS, columns, m), F32),
            pltpu.VMEM((LEVELS, columns, m), F32),
            pltpu.VMEM((m, columns), F32),
            pltpu.VMEM((columns, m), F32),
            pltpu.VMEM((m, m), BF16),
            pltpu.VMEM((m, m), BF16),
            pltpu.VMEM((m, m), BF16),
            pltpu.VMEM((m, m), BF16),
            pltpu.VMEM((m, m), BF16),
            pltpu.VMEM((m, m), BF16),
            pltpu.SemaphoreType.DMA((4,)),
            pltpu.SemaphoreType.DMA((copies,)),
            pltpu.SemaphoreType.DMA((copies,)),
        ],
        compiler_params=pltpu.CompilerParams(
            collective_id=0, has_side_effects=True, vmem_limit_bytes=56 * 2**20),
        name="reduction",
    )(diag_blocks[0].T, lower_blocks[0].T, upper_blocks[0].T, sources[0])
    return center.T[None], source[None]


def solution(mesh):
    placed = P("sec", None, "ch")
    return jax.shard_map(
        functools.partial(shards, mesh.shape["sec"]),
        mesh=mesh,
        in_specs=(placed,) * 4,
        out_specs=(placed, placed),
        check_vma=False,
    )
```

```python
import functools

import jax
import jax.numpy as jnp
from jax import lax
from jax.experimental import pallas as pl
from jax.experimental.pallas import tpu as pltpu
from jax.sharding import PartitionSpec as P

LEVELS = 3
NEAR, FAR = 0, 1
MESH = pl.DeviceIdType.MESH
F32 = jnp.float32
BF16 = jnp.bfloat16


def split(x):
    hi = x.astype(BF16)
    return hi, (x - hi.astype(F32)).astype(BF16)


def dot(a, b):
    return jnp.dot(a, b, preferred_element_type=F32)


def product(left, hi, lo):
    left_hi, left_lo = split(left)
    return dot(left_hi, hi) + (dot(left_lo, hi) + dot(left_hi, lo))


class Slots:
    def __init__(self):
        self.taken = {}

    def __call__(self, *name):
        return self.taken.setdefault(name, len(self.taken))


def kernel(sectors, m, a_in, l_in, u_in, b_in, a_out, b_out,
           wa, wc, zq, zwhole, rwhole, rq, zb, rb, b_raw, source,
           inv_hi, inv_lo, c_hi, c_lo, load_sem, ssem, rsem):
    sec = lax.axis_index("sec")
    ch = lax.axis_index("ch")
    z, y = ch // 4, ch % 4
    core = sec % 2
    toward = 1 - 2 * core
    side = 1 - 2 * ((sec % 8) // 4)
    quarter = m // 4
    half_rows = source.shape[0] // 2
    chunk = source.shape[0] // 4

    loads = [
        pltpu.make_async_copy(a_in, wa.at[0, z, y], load_sem.at[0]),
        pltpu.make_async_copy(l_in, wc.at[1 - core, 0, z, y], load_sem.at[1]),
        pltpu.make_async_copy(u_in, wc.at[core, 0, z, y], load_sem.at[2]),
        pltpu.make_async_copy(b_in, b_raw, load_sem.at[3]),
    ]
    for load in loads:
        load.start()

    def zat(d):
        return (z + d) % 4

    def yat(d):
        return (y + d) % 4

    def inside(index):
        return jnp.logical_and(index >= 0, index < sectors)

    z_next, z_prev = (sec, zat(1) * 4 + y), (sec, zat(3) * 4 + y)
    y_next, y_prev, y_far = (sec, z * 4 + yat(1)), (sec, z * 4 + yat(3)), (sec, z * 4 + yat(2))
    near = [sec + toward * 2 ** k for k in range(LEVELS)]
    far = [sec - toward * 2 ** k for k in range(LEVELS)]
    has_near = [inside(i) for i in near]
    has_far = [inside(i) for i in far]
    mirror, onward, backward = sec + 4 * side, sec + 8 * side, sec - 8 * side
    has_onward, has_backward = inside(onward), inside(backward)

    barrier = pltpu.get_barrier_semaphore()

    def greet(device):
        pl.semaphore_signal(barrier, inc=1, device_id=device, device_id_type=MESH)

    for device in (z_next, z_prev, y_next, y_prev, y_far):
        greet(device)
    peers = 5
    for index, there in zip(near + far + [onward, backward], has_near + has_far + [has_onward, has_backward]):
        @pl.when(there)
        def _():
            greet((index, ch))

        peers = peers + there.astype(jnp.int32)
    pl.semaphore_wait(barrier, peers)
    for load in loads:
        load.wait()

    slots = Slots()
    sent = []

    def copy(src, dst, index, device):
        return pltpu.make_async_remote_copy(
            src_ref=src, dst_ref=dst, send_sem=ssem.at[index], recv_sem=rsem.at[index],
            device_id=device, device_id_type=MESH)

    def push(ref, name, device):
        out = copy(ref, ref, slots(*name), device)
        out.start()
        sent.append((None, out))

    def arrived(ref, name):
        copy(ref, ref, slots(*name), y_next).wait_recv()

    def shift(there, src, dst, name, target):
        out = copy(src, dst, slots(*name), (target, ch))

        @pl.when(there)
        def _():
            out.start()

        sent.append((there, out))

    def shifted(there, ref, name):
        @pl.when(there)
        def _():
            arrived(ref, name)

    whole = (wa.at[0], wc.at[FAR, 0], wc.at[NEAR, 0])

    def slab(i, dz, dy):
        return whole[i].at[zat(dz), yat(dy)]

    def half(i, dz, part):
        return whole[i].at[zat(dz), y, pl.ds(16 * part, 16)]

    def z_own(i):
        push(slab(i, 0, 0), ("z", i, 1), z_next)
        push(slab(i, 0, 0), ("z", i, 3), z_prev)

    def y_send(i, r):
        push(slab(i, r, 0), ("y", i, r, 1), y_next)
        push(slab(i, r, 0), ("y", i, r, 3), y_prev)

    def z_relay(i):
        arrived(slab(i, 3, 0), ("z", i, 1))
        push(half(i, 3, 0), ("zz", i, 1), z_next)
        arrived(slab(i, 1, 0), ("z", i, 3))
        push(half(i, 1, 1), ("zz", i, 3), z_prev)
        y_send(i, 3)
        y_send(i, 1)

    def z_last(i):
        arrived(half(i, 2, 0), ("zz", i, 1))
        arrived(half(i, 2, 1), ("zz", i, 3))
        y_send(i, 2)

    def y_relay(i, r):
        arrived(slab(i, r, 3), ("y", i, r, 1))
        if r % 2 == 0:
            push(slab(i, r, 3), ("yy", i, r), y_next)
        arrived(slab(i, r, 1), ("y", i, r, 3))
        if r % 2 == 1:
            push(slab(i, r, 1), ("yy", i, r), y_prev)

    def y_last(i):
        for r in range(4):
            arrived(slab(i, r, 2), ("yy", i, r))

    def part(ref, dy, p):
        return ref.at[pl.ds(2 * p, 2), yat(dy)]

    def ring_start(ref, k):
        push(part(ref, 0, 0), ("r", k, 0), y_next)
        push(part(ref, 0, 1), ("r", k, 1), y_prev)
        push(part(ref, 0, 1), ("r", k, 2), y_next)
        push(part(ref, 0, 0), ("r", k, 3), y_prev)

    def ring_relay(ref, k):
        arrived(part(ref, 3, 0), ("r", k, 0))
        push(part(ref, 3, 0), ("r", k, 4), y_next)
        arrived(part(ref, 1, 1), ("r", k, 1))
        push(part(ref, 1, 1), ("r", k, 5), y_prev)

    def ring_end(ref, k):
        arrived(part(ref, 3, 1), ("r", k, 2))
        arrived(part(ref, 1, 0), ("r", k, 3))
        arrived(part(ref, 2, 0), ("r", k, 4))
        arrived(part(ref, 2, 1), ("r", k, 5))

    def spread(ref, k, role):
        push(ref.at[:, y], ("s", k, role, 1), y_next)
        push(ref.at[:, y], ("s", k, role, 3), y_prev)
        push(ref.at[:, y], ("s", k, role, 2), y_far)

    def spread_end(ref, k, role):
        arrived(ref.at[:, yat(3)], ("s", k, role, 1))
        arrived(ref.at[:, yat(1)], ("s", k, role, 3))
        arrived(ref.at[:, yat(2)], ("s", k, role, 2))

    def rows(ref):
        return ref[...].reshape(m, m)

    def own(ref):
        return ref[:, y].reshape(quarter, m)

    def put(ref, value):
        ref[:, y] = value.reshape(4, quarter // 4, m)

    def invert(k):
        block = rows(wa.at[k])
        on = lax.broadcasted_iota(jnp.int32, (m, m), 0) == lax.broadcasted_iota(jnp.int32, (m, m), 1)
        diag = jnp.where(on, block, 0.0)
        across = 1.0 / jnp.sum(diag, axis=0, keepdims=True)
        down = 1.0 / jnp.sum(diag, axis=1, keepdims=True)
        start = jnp.where(on, across, -(down * block * across))
        block_hi, block_lo = split(block)
        start_hi, start_lo = split(start)
        inner = product(start, block_hi, block_lo)
        inv_hi[...], inv_lo[...] = split(2.0 * start - product(inner, start_hi, start_lo))

    def solve(value):
        return product(value, inv_hi[...], inv_lo[...])

    def couple(value, role):
        return product(value, c_hi[role], c_lo[role])

    def hold(k, role):
        c_hi[role], c_lo[role] = split(rows(wc.at[role, k]))

    def update_source(k):
        shifted(has_near[k], rb.at[k, NEAR], ("b", k, NEAR))
        shifted(has_far[k], rb.at[k, FAR], ("b", k, FAR))
        source[...] = source[...] - couple(rb[k, NEAR], NEAR) - couple(rb[k, FAR], FAR)

    z_own(0)
    z_own(1)
    y_send(0, 0)
    y_send(1, 0)
    y_send(2, 0)
    source[...] = b_raw[...].T

    def clear(there, ref):
        @pl.when(jnp.logical_not(there))
        def _():
            ref[...] = jnp.zeros_like(ref)

    clear(has_far[0], rq.at[0, FAR])
    clear(has_far[0], rb.at[0, FAR])
    for k in range(1, LEVELS):
        clear(has_near[k], rq.at[k, NEAR])
        clear(has_far[k], rq.at[k, FAR])
    clear(has_near[1], rb.at[1, NEAR])
    clear(has_far[1], rb.at[1, FAR])
    clear(has_backward, rb.at[2, 1])
    z_relay(0)
    z_own(2)
    y_relay(0, 0)
    y_relay(1, 0)
    y_relay(2, 0)
    y_relay(0, 1)
    y_relay(0, 3)
    z_relay(1)
    z_last(0)
    y_relay(1, 1)
    y_relay(1, 3)
    y_relay(0, 2)
    z_relay(2)
    z_last(1)
    y_relay(2, 1)
    y_relay(2, 3)

    y_last(0)
    invert(0)
    y_relay(1, 2)
    z_last(2)
    y_relay(2, 2)
    zq[0, FAR] = solve(own(wc.at[FAR, 0]))
    shift(has_far[0], zq.at[0, FAR], rq.at[0, FAR, FAR], ("q", 0, FAR, FAR), far[0])
    zq[0, NEAR] = solve(own(wc.at[NEAR, 0]))
    shift(has_near[0], zq.at[0, NEAR], rq.at[0, NEAR, NEAR], ("q", 0, NEAR, NEAR), near[0])
    shift(has_far[0], zq.at[0, NEAR], rq.at[0, FAR, NEAR], ("q", 0, FAR, NEAR), far[0])
    zb[0] = solve(source[...])
    shift(has_far[0], zb.at[0], rb.at[0, FAR], ("b", 0, FAR), far[0])
    shift(has_near[0], zb.at[0], rb.at[0, NEAR], ("b", 0, NEAR), near[0])
    y_last(1)
    hold(0, FAR)
    shifted(has_far[0], rq.at[0, FAR, FAR], ("q", 0, FAR, FAR))
    center = own(wa.at[0]) - couple(rq[0, FAR, FAR], FAR)
    y_last(2)
    hold(0, NEAR)
    shifted(has_near[0], rq.at[0, NEAR, NEAR], ("q", 0, NEAR, NEAR))
    put(wa.at[1], center - couple(rq[0, NEAR, NEAR], NEAR))
    ring_start(wa.at[1], 1)
    zwhole[...] = solve(rows(wc.at[FAR, 0]))
    shift(has_near[0], zwhole, rwhole, ("w",), near[0])
    shifted(has_far[0], rq.at[0, FAR, NEAR], ("q", 0, FAR, NEAR))
    put(wc.at[FAR, 1], -couple(rq[0, FAR, NEAR], FAR))
    ring_relay(wa.at[1], 1)
    spread(wc.at[FAR, 1], 1, FAR)
    shifted(has_near[0], rwhole, ("w",))
    wc[NEAR, 1] = (-couple(rwhole[...], NEAR)).reshape(4, 4, quarter // 4, m)
    update_source(0)

    ring_end(wa.at[1], 1)
    invert(1)
    zq[1, NEAR] = solve(own(wc.at[NEAR, 1]))
    shift(has_near[1], zq.at[1, NEAR], rq.at[1, FAR, NEAR], ("q", 1, FAR, NEAR), near[1])
    zq[1, FAR] = solve(own(wc.at[FAR, 1]))
    shift(has_far[1], zq.at[1, FAR], rq.at[1, NEAR, FAR], ("q", 1, NEAR, FAR), far[1])
    shift(has_near[1], zq.at[1, FAR], rq.at[1, FAR, FAR], ("q", 1, FAR, FAR), near[1])
    shift(has_far[1], zq.at[1, NEAR], rq.at[1, NEAR, NEAR], ("q", 1, NEAR, NEAR), far[1])
    zb[1] = solve(source[...])
    shift(has_near[1], zb.at[1], rb.at[1, FAR], ("b", 1, FAR), near[1])
    shift(has_far[1], zb.at[1], rb.at[1, NEAR], ("b", 1, NEAR), far[1])
    hold(1, NEAR)
    spread_end(wc.at[FAR, 1], 1, FAR)
    hold(1, FAR)
    shifted(has_near[1], rq.at[1, NEAR, FAR], ("q", 1, NEAR, FAR))
    shifted(has_far[1], rq.at[1, FAR, NEAR], ("q", 1, FAR, NEAR))
    put(wa.at[2], own(wa.at[1]) - couple(rq[1, NEAR, FAR], NEAR) - couple(rq[1, FAR, NEAR], FAR))
    ring_start(wa.at[2], 2)
    shifted(has_near[1], rq.at[1, NEAR, NEAR], ("q", 1, NEAR, NEAR))
    put(wc.at[NEAR, 2], -couple(rq[1, NEAR, NEAR], NEAR))
    shifted(has_far[1], rq.at[1, FAR, FAR], ("q", 1, FAR, FAR))
    put(wc.at[FAR, 2], -couple(rq[1, FAR, FAR], FAR))
    ring_relay(wa.at[2], 2)
    spread(wc.at[NEAR, 2], 2, NEAR)
    spread(wc.at[FAR, 2], 2, FAR)

    ring_end(wa.at[2], 2)
    invert(2)
    zq[2, NEAR, 0:32] = solve(wc[NEAR, 2, z, y])
    shift(has_near[2], zq.at[2, NEAR, pl.ds(0, 32)], rq.at[2, FAR, NEAR, pl.ds(0, 32)], ("q", 2, FAR), near[2])
    zq[2, FAR, 0:32] = solve(wc[FAR, 2, z, y])
    shift(has_far[2], zq.at[2, FAR, pl.ds(0, 32)], rq.at[2, NEAR, FAR, pl.ds(0, 32)], ("q", 2, NEAR), far[2])
    update_source(1)
    always = mirror >= 0
    for c in range(4):
        if c % 2 == 0:
            here = pl.ds(chunk * c, half_rows)
            zb[2, here] = solve(source[here])
        here = pl.ds(chunk * c, chunk)
        shift(always, zb.at[2, here], rb.at[2, 0, here], ("c", c), mirror)
    spread_end(wc.at[NEAR, 2], 2, NEAR)
    hold(2, NEAR)
    spread_end(wc.at[FAR, 2], 2, FAR)
    hold(2, FAR)
    shifted(has_near[2], rq.at[2, NEAR, FAR, pl.ds(0, 32)], ("q", 2, NEAR))
    shifted(has_far[2], rq.at[2, FAR, NEAR, pl.ds(0, 32)], ("q", 2, FAR))
    a_out[...] = wa[2, z, y] - couple(rq[2, NEAR, FAR, 0:32], NEAR) - couple(rq[2, FAR, NEAR, 0:32], FAR)
    direct = (1 - toward * side) // 2
    for c in range(4):
        here = pl.ds(chunk * c, chunk)
        arrived(rb.at[2, 0, here], ("c", c))
        shift(has_onward, rb.at[2, 0, here], rb.at[2, 1, here], ("d", c), onward)
        if c % 2 == 1:
            here = pl.ds(chunk * (c - 1), half_rows)
            source[here] = source[here] - couple(rb[2, 0, here], direct)
    for c in range(4):
        shifted(has_backward, rb.at[2, 1, pl.ds(chunk * c, chunk)], ("d", c))
        if c % 2 == 1:
            here = pl.ds(chunk * (c - 1), half_rows)
            source[here] = source[here] - couple(rb[2, 1, here], 1 - direct)
    b_out[...] = source[...].T

    for there, out in sent:
        if there is None:
            out.wait_send()
        else:
            pl.when(there)(out.wait_send)


def shards(sectors, diag_blocks, lower_blocks, upper_blocks, sources):
    m = diag_blocks.shape[1]
    width = diag_blocks.shape[2]
    columns = sources.shape[2]
    quarter = m // 4
    copies = 128
    vmem = pl.BlockSpec(memory_space=pltpu.VMEM)
    hbm = pl.BlockSpec(memory_space=pl.ANY)
    center, source = pl.pallas_call(
        functools.partial(kernel, sectors, m),
        out_shape=(jax.ShapeDtypeStruct((width, m), F32), jax.ShapeDtypeStruct((m, columns), F32)),
        in_specs=[hbm] * 4,
        out_specs=(vmem, vmem),
        scratch_shapes=[
            pltpu.VMEM((LEVELS, 4, 4, width, m), F32),
            pltpu.VMEM((2, LEVELS, 4, 4, width, m), F32),
            pltpu.VMEM((LEVELS, 2, quarter, m), F32),
            pltpu.VMEM((m, m), F32),
            pltpu.VMEM((m, m), F32),
            pltpu.VMEM((LEVELS, 2, 2, quarter, m), F32),
            pltpu.VMEM((LEVELS, columns, m), F32),
            pltpu.VMEM((LEVELS, 2, columns, m), F32),
            pltpu.VMEM((m, columns), F32),
            pltpu.VMEM((columns, m), F32),
            pltpu.VMEM((m, m), BF16),
            pltpu.VMEM((m, m), BF16),
            pltpu.VMEM((2, m, m), BF16),
            pltpu.VMEM((2, m, m), BF16),
            pltpu.SemaphoreType.DMA((4,)),
            pltpu.SemaphoreType.DMA((copies,)),
            pltpu.SemaphoreType.DMA((copies,)),
        ],
        compiler_params=pltpu.CompilerParams(
            collective_id=0, has_side_effects=True, vmem_limit_bytes=56 * 2**20),
        name="reduction",
    )(diag_blocks[0].T, lower_blocks[0].T, upper_blocks[0].T, sources[0])
    return center.T[None], source[None]


def solution(mesh):
    placed = P("sec", None, "ch")
    return jax.shard_map(
        functools.partial(shards, mesh.shape["sec"]),
        mesh=mesh,
        in_specs=(placed,) * 4,
        out_specs=(placed, placed),
        check_vma=False,
    )
```

```python
import functools

import jax
import jax.numpy as jnp
from jax import lax
from jax.experimental import pallas as pl
from jax.experimental.pallas import tpu as pltpu
from jax.sharding import PartitionSpec as P

LEVELS = 3
NEAR, FAR = 0, 1
MESH = pl.DeviceIdType.MESH
F32 = jnp.float32
BF16 = jnp.bfloat16


def split(x):
    hi = x.astype(BF16)
    return hi, (x - hi.astype(F32)).astype(BF16)


def dot(a, b):
    return jnp.dot(a, b, preferred_element_type=F32)


def product(left, hi, lo):
    left_hi, left_lo = split(left)
    return dot(left_hi, hi) + (dot(left_lo, hi) + dot(left_hi, lo))


class Slots:
    def __init__(self):
        self.taken = {}

    def __call__(self, *name):
        return self.taken.setdefault(name, len(self.taken))


def kernel(sectors, m, a_in, l_in, u_in, b_in, a_out, b_out,
           wa, wc, zq, zwhole, rwhole, rq, zb, rb, b_raw, source,
           inv_hi, inv_lo, c_hi, c_lo, load_sem, ssem, rsem):
    sec = lax.axis_index("sec")
    ch = lax.axis_index("ch")
    z, y = ch // 4, ch % 4
    core = sec % 2
    toward = 1 - 2 * core
    side = 1 - 2 * ((sec % 8) // 4)
    quarter = m // 4
    half_rows = source.shape[0] // 2
    chunk = source.shape[0] // 4

    loads = [
        pltpu.make_async_copy(a_in, wa.at[0, z, y], load_sem.at[0]),
        pltpu.make_async_copy(l_in, wc.at[1 - core, 0, z, y], load_sem.at[1]),
        pltpu.make_async_copy(u_in, wc.at[core, 0, z, y], load_sem.at[2]),
        pltpu.make_async_copy(b_in, b_raw, load_sem.at[3]),
    ]
    for load in loads:
        load.start()

    def zat(d):
        return (z + d) % 4

    def yat(d):
        return (y + d) % 4

    def inside(index):
        return jnp.logical_and(index >= 0, index < sectors)

    z_next, z_prev = (sec, zat(1) * 4 + y), (sec, zat(3) * 4 + y)
    y_next, y_prev, y_far = (sec, z * 4 + yat(1)), (sec, z * 4 + yat(3)), (sec, z * 4 + yat(2))
    near = [sec + toward * 2 ** k for k in range(LEVELS)]
    far = [sec - toward * 2 ** k for k in range(LEVELS)]
    has_near = [inside(i) for i in near]
    has_far = [inside(i) for i in far]
    mirror, onward, backward = sec + 4 * side, sec + 8 * side, sec - 8 * side
    has_onward, has_backward = inside(onward), inside(backward)

    barrier = pltpu.get_barrier_semaphore()

    def greet(device):
        pl.semaphore_signal(barrier, inc=1, device_id=device, device_id_type=MESH)

    for device in (z_next, z_prev, y_next, y_prev, y_far):
        greet(device)
    peers = 5
    for index, there in zip(near + far + [onward, backward], has_near + has_far + [has_onward, has_backward]):
        @pl.when(there)
        def _():
            greet((index, ch))

        peers = peers + there.astype(jnp.int32)
    pl.semaphore_wait(barrier, peers)
    for load in loads:
        load.wait()

    slots = Slots()
    sent = []

    def copy(src, dst, index, device):
        return pltpu.make_async_remote_copy(
            src_ref=src, dst_ref=dst, send_sem=ssem.at[index], recv_sem=rsem.at[index],
            device_id=device, device_id_type=MESH)

    def push(ref, name, device):
        out = copy(ref, ref, slots(*name), device)
        out.start()
        sent.append((None, out))

    def arrived(ref, name):
        copy(ref, ref, slots(*name), y_next).wait_recv()

    def shift(there, src, dst, name, target):
        out = copy(src, dst, slots(*name), (target, ch))

        @pl.when(there)
        def _():
            out.start()

        sent.append((there, out))

    def shifted(there, ref, name):
        @pl.when(there)
        def _():
            arrived(ref, name)

    whole = (wa.at[0], wc.at[FAR, 0], wc.at[NEAR, 0])

    def slab(i, dz, dy):
        return whole[i].at[zat(dz), yat(dy)]

    def half(i, dz, part):
        return whole[i].at[zat(dz), y, pl.ds(16 * part, 16)]

    def z_own(i):
        push(slab(i, 0, 0), ("z", i, 1), z_next)
        push(slab(i, 0, 0), ("z", i, 3), z_prev)

    def y_send(i, r):
        push(slab(i, r, 0), ("y", i, r, 1), y_next)
        push(slab(i, r, 0), ("y", i, r, 3), y_prev)
        push(slab(i, r, 0), ("y", i, r, 2), y_far)

    def z_relay(i):
        arrived(slab(i, 3, 0), ("z", i, 1))
        push(half(i, 3, 0), ("zz", i, 1), z_next)
        arrived(slab(i, 1, 0), ("z", i, 3))
        push(half(i, 1, 1), ("zz", i, 3), z_prev)
        y_send(i, 3)
        y_send(i, 1)

    def z_last(i):
        arrived(half(i, 2, 0), ("zz", i, 1))
        arrived(half(i, 2, 1), ("zz", i, 3))
        y_send(i, 2)

    def y_last(i):
        for r in range(4):
            arrived(slab(i, r, 3), ("y", i, r, 1))
            arrived(slab(i, r, 1), ("y", i, r, 3))
            arrived(slab(i, r, 2), ("y", i, r, 2))

    def part(ref, dy, p):
        return ref.at[pl.ds(2 * p, 2), yat(dy)]

    def ring_start(ref, *tag):
        push(part(ref, 0, 0), ("r", *tag, 0), y_next)
        push(part(ref, 0, 1), ("r", *tag, 1), y_prev)
        push(part(ref, 0, 1), ("r", *tag, 2), y_next)
        push(part(ref, 0, 0), ("r", *tag, 3), y_prev)

    def ring_relay(ref, *tag):
        arrived(part(ref, 3, 0), ("r", *tag, 0))
        push(part(ref, 3, 0), ("r", *tag, 4), y_next)
        arrived(part(ref, 1, 1), ("r", *tag, 1))
        push(part(ref, 1, 1), ("r", *tag, 5), y_prev)

    def ring_end(ref, *tag):
        arrived(part(ref, 3, 1), ("r", *tag, 2))
        arrived(part(ref, 1, 0), ("r", *tag, 3))
        arrived(part(ref, 2, 0), ("r", *tag, 4))
        arrived(part(ref, 2, 1), ("r", *tag, 5))

    def rows(ref):
        return ref[...].reshape(m, m)

    def own(ref):
        return ref[:, y].reshape(quarter, m)

    def put(ref, value):
        ref[:, y] = value.reshape(4, quarter // 4, m)

    def invert(k):
        block = rows(wa.at[k])
        on = lax.broadcasted_iota(jnp.int32, (m, m), 0) == lax.broadcasted_iota(jnp.int32, (m, m), 1)
        diag = jnp.where(on, block, 0.0)
        across = 1.0 / jnp.sum(diag, axis=0, keepdims=True)
        down = 1.0 / jnp.sum(diag, axis=1, keepdims=True)
        start = jnp.where(on, across, -(down * block * across))
        block_hi, block_lo = split(block)
        start_hi, start_lo = split(start)
        inner = product(start, block_hi, block_lo)
        inv_hi[...], inv_lo[...] = split(2.0 * start - product(inner, start_hi, start_lo))

    def solve(value):
        return product(value, inv_hi[...], inv_lo[...])

    def couple(value, role):
        return product(value, c_hi[role], c_lo[role])

    def hold(k, role):
        c_hi[role], c_lo[role] = split(rows(wc.at[role, k]))

    z_own(0)
    z_own(1)
    y_send(0, 0)
    y_send(1, 0)
    y_send(2, 0)
    source[...] = b_raw[...].T

    def clear(there, ref):
        @pl.when(jnp.logical_not(there))
        def _():
            ref[...] = jnp.zeros_like(ref)

    clear(has_far[0], rq.at[0, FAR])
    clear(has_far[0], rb.at[0, FAR])
    for k in range(1, LEVELS):
        clear(has_near[k], rq.at[k, NEAR])
        clear(has_far[k], rq.at[k, FAR])
    clear(has_near[1], rb.at[1, NEAR])
    clear(has_far[1], rb.at[1, FAR])
    clear(has_backward, rb.at[2, 1])
    z_relay(0)
    z_own(2)
    z_relay(1)
    z_last(0)
    z_relay(2)
    z_last(1)
    z_last(2)

    y_last(0)
    invert(0)
    zq[0, FAR] = solve(own(wc.at[FAR, 0]))
    shift(has_far[0], zq.at[0, FAR], rq.at[0, FAR, FAR], ("q", 0, FAR, FAR), far[0])
    zq[0, NEAR] = solve(own(wc.at[NEAR, 0]))
    shift(has_near[0], zq.at[0, NEAR], rq.at[0, NEAR, NEAR], ("q", 0, NEAR, NEAR), near[0])
    zb[0] = solve(source[...])
    y_last(1)
    hold(0, FAR)
    shifted(has_far[0], rq.at[0, FAR, FAR], ("q", 0, FAR, FAR))
    shift(has_far[0], zq.at[0, NEAR], rq.at[0, FAR, NEAR], ("q", 0, FAR, NEAR), far[0])
    center = own(wa.at[0]) - couple(rq[0, FAR, FAR], FAR)
    y_last(2)
    hold(0, NEAR)
    shifted(has_near[0], rq.at[0, NEAR, NEAR], ("q", 0, NEAR, NEAR))
    put(wa.at[1], center - couple(rq[0, NEAR, NEAR], NEAR))
    ring_start(wa.at[1], 1)
    shift(has_far[0], zb.at[0], rb.at[0, FAR], ("b", 0, FAR), far[0])
    shift(has_near[0], zb.at[0], rb.at[0, NEAR], ("b", 0, NEAR), near[0])
    zwhole[...] = solve(rows(wc.at[FAR, 0]))
    shift(has_near[0], zwhole, rwhole, ("w",), near[0])
    shifted(has_far[0], rq.at[0, FAR, NEAR], ("q", 0, FAR, NEAR))
    put(wc.at[FAR, 1], -couple(rq[0, FAR, NEAR], FAR))
    ring_relay(wa.at[1], 1)
    ring_start(wc.at[FAR, 1], 1, FAR)
    shifted(has_near[0], rwhole, ("w",))
    wc[NEAR, 1] = (-couple(rwhole[...], NEAR)).reshape(4, 4, quarter // 4, m)
    shifted(has_near[0], rb.at[0, NEAR], ("b", 0, NEAR))
    shifted(has_far[0], rb.at[0, FAR], ("b", 0, FAR))
    source[...] = source[...] - couple(rb[0, NEAR], NEAR) - couple(rb[0, FAR], FAR)

    ring_end(wa.at[1], 1)
    ring_relay(wc.at[FAR, 1], 1, FAR)
    invert(1)
    zq[1, NEAR] = solve(own(wc.at[NEAR, 1]))
    shift(has_near[1], zq.at[1, NEAR], rq.at[1, FAR, NEAR], ("q", 1, FAR, NEAR), near[1])
    zq[1, FAR] = solve(own(wc.at[FAR, 1]))
    shift(has_far[1], zq.at[1, FAR], rq.at[1, NEAR, FAR], ("q", 1, NEAR, FAR), far[1])
    zb[1] = solve(source[...])
    hold(1, NEAR)
    ring_end(wc.at[FAR, 1], 1, FAR)
    hold(1, FAR)
    shifted(has_near[1], rq.at[1, NEAR, FAR], ("q", 1, NEAR, FAR))
    shifted(has_far[1], rq.at[1, FAR, NEAR], ("q", 1, FAR, NEAR))
    shift(has_near[1], zq.at[1, FAR], rq.at[1, FAR, FAR], ("q", 1, FAR, FAR), near[1])
    shift(has_far[1], zq.at[1, NEAR], rq.at[1, NEAR, NEAR], ("q", 1, NEAR, NEAR), far[1])
    put(wa.at[2], own(wa.at[1]) - couple(rq[1, NEAR, FAR], NEAR) - couple(rq[1, FAR, NEAR], FAR))
    ring_start(wa.at[2], 2)

    def halves(h):
        return pl.ds(half_rows * h, half_rows)

    def send_half(h):
        shift(has_near[1], zb.at[1, halves(h)], rb.at[1, FAR, halves(h)], ("b", 1, FAR, h), near[1])
        shift(has_far[1], zb.at[1, halves(h)], rb.at[1, NEAR, halves(h)], ("b", 1, NEAR, h), far[1])

    ring_relay(wa.at[2], 2)
    send_half(0)
    shifted(has_near[1], rq.at[1, NEAR, NEAR], ("q", 1, NEAR, NEAR))
    put(wc.at[NEAR, 2], -couple(rq[1, NEAR, NEAR], NEAR))
    ring_start(wc.at[NEAR, 2], 2, NEAR)
    shifted(has_far[1], rq.at[1, FAR, FAR], ("q", 1, FAR, FAR))
    put(wc.at[FAR, 2], -couple(rq[1, FAR, FAR], FAR))
    ring_start(wc.at[FAR, 2], 2, FAR)
    send_half(1)

    ring_end(wa.at[2], 2)
    invert(2)
    zq[2, NEAR, 0:32] = solve(wc[NEAR, 2, z, y])
    shift(has_near[2], zq.at[2, NEAR, pl.ds(0, 32)], rq.at[2, FAR, NEAR, pl.ds(0, 32)], ("q", 2, FAR), near[2])
    zq[2, FAR, 0:32] = solve(wc[FAR, 2, z, y])
    shift(has_far[2], zq.at[2, FAR, pl.ds(0, 32)], rq.at[2, NEAR, FAR, pl.ds(0, 32)], ("q", 2, NEAR), far[2])
    ring_relay(wc.at[NEAR, 2], 2, NEAR)
    ring_relay(wc.at[FAR, 2], 2, FAR)
    always = mirror >= 0
    for h in range(2):
        here = halves(h)
        shifted(has_near[1], rb.at[1, NEAR, here], ("b", 1, NEAR, h))
        shifted(has_far[1], rb.at[1, FAR, here], ("b", 1, FAR, h))
        source[here] = source[here] - couple(rb[1, NEAR, here], NEAR) - couple(rb[1, FAR, here], FAR)
        zb[2, here] = solve(source[here])
        for c in (2 * h, 2 * h + 1):
            there = pl.ds(chunk * c, chunk)
            shift(always, zb.at[2, there], rb.at[2, 0, there], ("c", c), mirror)
    ring_end(wc.at[NEAR, 2], 2, NEAR)
    hold(2, NEAR)
    ring_end(wc.at[FAR, 2], 2, FAR)
    hold(2, FAR)
    shifted(has_near[2], rq.at[2, NEAR, FAR, pl.ds(0, 32)], ("q", 2, NEAR))
    shifted(has_far[2], rq.at[2, FAR, NEAR, pl.ds(0, 32)], ("q", 2, FAR))
    a_out[...] = wa[2, z, y] - couple(rq[2, NEAR, FAR, 0:32], NEAR) - couple(rq[2, FAR, NEAR, 0:32], FAR)
    direct = (1 - toward * side) // 2
    for c in range(4):
        here = pl.ds(chunk * c, chunk)
        arrived(rb.at[2, 0, here], ("c", c))
        shift(has_onward, rb.at[2, 0, here], rb.at[2, 1, here], ("d", c), onward)
        if c % 2 == 1:
            here = halves(c // 2)
            source[here] = source[here] - couple(rb[2, 0, here], direct)
    for c in range(4):
        shifted(has_backward, rb.at[2, 1, pl.ds(chunk * c, chunk)], ("d", c))
        if c % 2 == 1:
            here = halves(c // 2)
            source[here] = source[here] - couple(rb[2, 1, here], 1 - direct)
    b_out[...] = source[...].T

    for there, out in sent:
        if there is None:
            out.wait_send()
        else:
            pl.when(there)(out.wait_send)


def shards(sectors, diag_blocks, lower_blocks, upper_blocks, sources):
    m = diag_blocks.shape[1]
    width = diag_blocks.shape[2]
    columns = sources.shape[2]
    quarter = m // 4
    copies = 128
    vmem = pl.BlockSpec(memory_space=pltpu.VMEM)
    hbm = pl.BlockSpec(memory_space=pl.ANY)
    center, source = pl.pallas_call(
        functools.partial(kernel, sectors, m),
        out_shape=(jax.ShapeDtypeStruct((width, m), F32), jax.ShapeDtypeStruct((m, columns), F32)),
        in_specs=[hbm] * 4,
        out_specs=(vmem, vmem),
        scratch_shapes=[
            pltpu.VMEM((LEVELS, 4, 4, width, m), F32),
            pltpu.VMEM((2, LEVELS, 4, 4, width, m), F32),
            pltpu.VMEM((LEVELS, 2, quarter, m), F32),
            pltpu.VMEM((m, m), F32),
            pltpu.VMEM((m, m), F32),
            pltpu.VMEM((LEVELS, 2, 2, quarter, m), F32),
            pltpu.VMEM((LEVELS, columns, m), F32),
            pltpu.VMEM((LEVELS, 2, columns, m), F32),
            pltpu.VMEM((m, columns), F32),
            pltpu.VMEM((columns, m), F32),
            pltpu.VMEM((m, m), BF16),
            pltpu.VMEM((m, m), BF16),
            pltpu.VMEM((2, m, m), BF16),
            pltpu.VMEM((2, m, m), BF16),
            pltpu.SemaphoreType.DMA((4,)),
            pltpu.SemaphoreType.DMA((copies,)),
            pltpu.SemaphoreType.DMA((copies,)),
        ],
        compiler_params=pltpu.CompilerParams(
            collective_id=0, has_side_effects=True, vmem_limit_bytes=56 * 2**20),
        name="reduction",
    )(diag_blocks[0].T, lower_blocks[0].T, upper_blocks[0].T, sources[0])
    return center.T[None], source[None]


def solution(mesh):
    placed = P("sec", None, "ch")
    return jax.shard_map(
        functools.partial(shards, mesh.shape["sec"]),
        mesh=mesh,
        in_specs=(placed,) * 4,
        out_specs=(placed, placed),
        check_vma=False,
    )
```

```python
import functools

import jax
import jax.numpy as jnp
from jax import lax
from jax.experimental import pallas as pl
from jax.experimental.pallas import tpu as pltpu
from jax.sharding import PartitionSpec as P

LEVELS = 3
NEAR, FAR = 0, 1
MESH = pl.DeviceIdType.MESH
F32 = jnp.float32
BF16 = jnp.bfloat16


def split(x):
    hi = x.astype(BF16)
    return hi, (x - hi.astype(F32)).astype(BF16)


def dot(a, b):
    return jnp.dot(a, b, preferred_element_type=F32)


def product(left, hi, lo):
    left_hi, left_lo = split(left)
    return dot(left_hi, hi) + (dot(left_lo, hi) + dot(left_hi, lo))


class Slots:
    def __init__(self):
        self.taken = {}

    def __call__(self, *name):
        return self.taken.setdefault(name, len(self.taken))


def kernel(sectors, m, a_in, l_in, u_in, b_in, a_out, b_out,
           wa, wc, zq, zwhole, rwhole, rq, zb, rb, b_raw, source,
           inv_hi, inv_lo, c_hi, c_lo, load_sem, ssem, rsem):
    sec = lax.axis_index("sec")
    ch = lax.axis_index("ch")
    z, y = ch // 4, ch % 4
    core = sec % 2
    toward = 1 - 2 * core
    side = 1 - 2 * ((sec % 8) // 4)
    quarter = m // 4
    half_rows = source.shape[0] // 2

    loads = [
        pltpu.make_async_copy(a_in, wa.at[0, z, y], load_sem.at[0]),
        pltpu.make_async_copy(l_in, wc.at[1 - core, 0, z, y], load_sem.at[1]),
        pltpu.make_async_copy(u_in, wc.at[core, 0, z, y], load_sem.at[2]),
        pltpu.make_async_copy(b_in, b_raw, load_sem.at[3]),
    ]
    for load in loads:
        load.start()

    def zat(d):
        return (z + d) % 4

    def yat(d):
        return (y + d) % 4

    def inside(index):
        return jnp.logical_and(index >= 0, index < sectors)

    z_next, z_prev = (sec, zat(1) * 4 + y), (sec, zat(3) * 4 + y)
    y_next, y_prev, y_far = (sec, z * 4 + yat(1)), (sec, z * 4 + yat(3)), (sec, z * 4 + yat(2))
    near = [sec + toward * 2 ** k for k in range(LEVELS)]
    far = [sec - toward * 2 ** k for k in range(LEVELS)]
    has_near = [inside(i) for i in near]
    has_far = [inside(i) for i in far]
    mirror, onward, backward = sec + 4 * side, sec + 8 * side, sec - 8 * side
    has_onward, has_backward = inside(onward), inside(backward)

    barrier = pltpu.get_barrier_semaphore()

    def greet(device):
        pl.semaphore_signal(barrier, inc=1, device_id=device, device_id_type=MESH)

    for device in (z_next, z_prev, y_next, y_prev, y_far):
        greet(device)
    peers = 5
    for index, there in zip(near + far + [onward, backward], has_near + has_far + [has_onward, has_backward]):
        @pl.when(there)
        def _():
            greet((index, ch))

        peers = peers + there.astype(jnp.int32)
    pl.semaphore_wait(barrier, peers)
    for load in loads:
        load.wait()

    slots = Slots()
    sent = []

    def copy(src, dst, index, device):
        return pltpu.make_async_remote_copy(
            src_ref=src, dst_ref=dst, send_sem=ssem.at[index], recv_sem=rsem.at[index],
            device_id=device, device_id_type=MESH)

    def push(ref, name, device):
        out = copy(ref, ref, slots(*name), device)
        out.start()
        sent.append((None, out))

    def arrived(ref, name):
        copy(ref, ref, slots(*name), y_next).wait_recv()

    def shift(there, src, dst, name, target):
        out = copy(src, dst, slots(*name), (target, ch))

        @pl.when(there)
        def _():
            out.start()

        sent.append((there, out))

    def shifted(there, ref, name):
        @pl.when(there)
        def _():
            arrived(ref, name)

    whole = (wa.at[0], wc.at[FAR, 0], wc.at[NEAR, 0])

    def slab(i, dz, dy):
        return whole[i].at[zat(dz), yat(dy)]

    def half(i, dz, part):
        return whole[i].at[zat(dz), y, pl.ds(16 * part, 16)]

    def z_own(i):
        push(slab(i, 0, 0), ("z", i, 1), z_next)
        push(slab(i, 0, 0), ("z", i, 3), z_prev)

    def y_send(i, r):
        push(slab(i, r, 0), ("y", i, r, 1), y_next)
        push(slab(i, r, 0), ("y", i, r, 3), y_prev)
        if r % 2 == 0:
            push(slab(i, r, 0), ("y", i, r, 2), y_far)

    def y_half(i, r, dy, part):
        return whole[i].at[zat(r), yat(dy), pl.ds(16 * part, 16)]

    def y_relay(i):
        for r in (3, 1):
            arrived(slab(i, r, 3), ("y", i, r, 1))
            push(y_half(i, r, 3, 0), ("yy", i, r, 1), y_next)
            arrived(slab(i, r, 1), ("y", i, r, 3))
            push(y_half(i, r, 1, 1), ("yy", i, r, 3), y_prev)

    def z_relay(i):
        arrived(slab(i, 3, 0), ("z", i, 1))
        push(half(i, 3, 0), ("zz", i, 1), z_next)
        arrived(slab(i, 1, 0), ("z", i, 3))
        push(half(i, 1, 1), ("zz", i, 3), z_prev)
        y_send(i, 3)
        y_send(i, 1)

    def z_last(i):
        arrived(half(i, 2, 0), ("zz", i, 1))
        arrived(half(i, 2, 1), ("zz", i, 3))
        y_send(i, 2)

    seen = set()

    def y_wait(i, r):
        if (i, r) not in seen:
            seen.add((i, r))
            arrived(slab(i, r, 3), ("y", i, r, 1))
            arrived(slab(i, r, 1), ("y", i, r, 3))

    def y_last(i):
        for r in (0, 2):
            y_wait(i, r)
            arrived(slab(i, r, 2), ("y", i, r, 2))
        for r in (1, 3):
            arrived(y_half(i, r, 2, 0), ("yy", i, r, 1))
            arrived(y_half(i, r, 2, 1), ("yy", i, r, 3))

    def part(ref, dy, p):
        return ref.at[pl.ds(2 * p, 2), yat(dy)]

    def ring_start(ref, *tag):
        push(part(ref, 0, 0), ("r", *tag, 0), y_next)
        push(part(ref, 0, 1), ("r", *tag, 1), y_prev)
        push(part(ref, 0, 1), ("r", *tag, 2), y_next)
        push(part(ref, 0, 0), ("r", *tag, 3), y_prev)

    def ring_relay(ref, *tag):
        arrived(part(ref, 3, 0), ("r", *tag, 0))
        push(part(ref, 3, 0), ("r", *tag, 4), y_next)
        arrived(part(ref, 1, 1), ("r", *tag, 1))
        push(part(ref, 1, 1), ("r", *tag, 5), y_prev)

    def ring_end(ref, *tag):
        arrived(part(ref, 3, 1), ("r", *tag, 2))
        arrived(part(ref, 1, 0), ("r", *tag, 3))
        arrived(part(ref, 2, 0), ("r", *tag, 4))
        arrived(part(ref, 2, 1), ("r", *tag, 5))

    def rows(ref):
        return ref[...].reshape(m, m)

    def own(ref):
        return ref[:, y].reshape(quarter, m)

    def put(ref, value):
        ref[:, y] = value.reshape(4, quarter // 4, m)

    def invert(k):
        block = rows(wa.at[k])
        on = lax.broadcasted_iota(jnp.int32, (m, m), 0) == lax.broadcasted_iota(jnp.int32, (m, m), 1)
        diag = jnp.where(on, block, 0.0)
        across = 1.0 / jnp.sum(diag, axis=0, keepdims=True)
        down = 1.0 / jnp.sum(diag, axis=1, keepdims=True)
        start = jnp.where(on, across, -(down * block * across))
        block_hi, block_lo = split(block)
        start_hi, start_lo = split(start)
        inner = product(start, block_hi, block_lo)
        inv_hi[...], inv_lo[...] = split(2.0 * start - product(inner, start_hi, start_lo))

    def solve(value):
        return product(value, inv_hi[...], inv_lo[...])

    def couple(value, role):
        return product(value, c_hi[role], c_lo[role])

    def hold(k, role):
        c_hi[role], c_lo[role] = split(rows(wc.at[role, k]))

    z_own(0)
    y_send(0, 0)
    y_send(1, 0)
    y_send(2, 0)
    source[...] = b_raw[...].T

    def clear(there, ref):
        @pl.when(jnp.logical_not(there))
        def _():
            ref[...] = jnp.zeros_like(ref)

    clear(has_far[0], rq.at[0, FAR])
    clear(has_far[0], rb.at[0, FAR])
    for k in range(1, LEVELS):
        clear(has_near[k], rq.at[k, NEAR])
        clear(has_far[k], rq.at[k, FAR])
    clear(has_near[1], rb.at[1, NEAR])
    clear(has_far[1], rb.at[1, FAR])
    clear(has_backward, rb.at[2, 1])
    y_wait(0, 0)
    z_own(1)
    z_relay(0)
    z_own(2)
    y_relay(0)
    z_relay(1)
    y_relay(1)
    z_last(0)
    z_relay(2)
    y_last(0)
    invert(0)
    z_last(1)
    y_relay(2)
    z_last(2)

    zq[0, FAR] = solve(own(wc.at[FAR, 0]))
    shift(has_far[0], zq.at[0, FAR], rq.at[0, FAR, FAR], ("q", 0, FAR, FAR), far[0])
    zq[0, NEAR] = solve(own(wc.at[NEAR, 0]))
    shift(has_near[0], zq.at[0, NEAR], rq.at[0, NEAR, NEAR], ("q", 0, NEAR, NEAR), near[0])
    zb[0] = solve(source[...])
    y_last(1)
    hold(0, FAR)
    shifted(has_far[0], rq.at[0, FAR, FAR], ("q", 0, FAR, FAR))
    shift(has_far[0], zq.at[0, NEAR], rq.at[0, FAR, NEAR], ("q", 0, FAR, NEAR), far[0])
    center = own(wa.at[0]) - couple(rq[0, FAR, FAR], FAR)
    y_last(2)
    hold(0, NEAR)
    shifted(has_near[0], rq.at[0, NEAR, NEAR], ("q", 0, NEAR, NEAR))
    put(wa.at[1], center - couple(rq[0, NEAR, NEAR], NEAR))
    ring_start(wa.at[1], 1)
    shift(has_far[0], zb.at[0], rb.at[0, FAR], ("b", 0, FAR), far[0])
    shift(has_near[0], zb.at[0], rb.at[0, NEAR], ("b", 0, NEAR), near[0])
    zwhole[...] = solve(rows(wc.at[FAR, 0]))
    shift(has_near[0], zwhole, rwhole, ("w",), near[0])
    shifted(has_far[0], rq.at[0, FAR, NEAR], ("q", 0, FAR, NEAR))
    put(wc.at[FAR, 1], -couple(rq[0, FAR, NEAR], FAR))
    ring_relay(wa.at[1], 1)
    ring_start(wc.at[FAR, 1], 1, FAR)
    shifted(has_near[0], rwhole, ("w",))
    wc[NEAR, 1] = (-couple(rwhole[...], NEAR)).reshape(4, 4, quarter // 4, m)
    shifted(has_near[0], rb.at[0, NEAR], ("b", 0, NEAR))
    shifted(has_far[0], rb.at[0, FAR], ("b", 0, FAR))
    source[...] = source[...] - couple(rb[0, NEAR], NEAR) - couple(rb[0, FAR], FAR)

    def halves(h):
        return pl.ds(half_rows * h, half_rows)

    def send_half(h):
        shift(has_near[1], zb.at[1, halves(h)], rb.at[1, FAR, halves(h)], ("b", 1, FAR, h), near[1])
        shift(has_far[1], zb.at[1, halves(h)], rb.at[1, NEAR, halves(h)], ("b", 1, NEAR, h), far[1])

    ring_end(wa.at[1], 1)
    ring_relay(wc.at[FAR, 1], 1, FAR)
    invert(1)
    zq[1, NEAR] = solve(own(wc.at[NEAR, 1]))
    shift(has_near[1], zq.at[1, NEAR], rq.at[1, FAR, NEAR], ("q", 1, FAR, NEAR), near[1])
    zq[1, FAR] = solve(own(wc.at[FAR, 1]))
    shift(has_far[1], zq.at[1, FAR], rq.at[1, NEAR, FAR], ("q", 1, NEAR, FAR), far[1])
    zb[1] = solve(source[...])
    hold(1, NEAR)
    ring_end(wc.at[FAR, 1], 1, FAR)
    hold(1, FAR)
    shifted(has_near[1], rq.at[1, NEAR, FAR], ("q", 1, NEAR, FAR))
    shifted(has_far[1], rq.at[1, FAR, NEAR], ("q", 1, FAR, NEAR))
    shift(has_near[1], zq.at[1, FAR], rq.at[1, FAR, FAR], ("q", 1, FAR, FAR), near[1])
    shift(has_far[1], zq.at[1, NEAR], rq.at[1, NEAR, NEAR], ("q", 1, NEAR, NEAR), far[1])
    put(wa.at[2], own(wa.at[1]) - couple(rq[1, NEAR, FAR], NEAR) - couple(rq[1, FAR, NEAR], FAR))
    ring_start(wa.at[2], 2)
    ring_relay(wa.at[2], 2)
    send_half(0)
    shifted(has_near[1], rq.at[1, NEAR, NEAR], ("q", 1, NEAR, NEAR))
    put(wc.at[NEAR, 2], -couple(rq[1, NEAR, NEAR], NEAR))
    ring_start(wc.at[NEAR, 2], 2, NEAR)
    shifted(has_far[1], rq.at[1, FAR, FAR], ("q", 1, FAR, FAR))
    put(wc.at[FAR, 2], -couple(rq[1, FAR, FAR], FAR))
    ring_start(wc.at[FAR, 2], 2, FAR)
    send_half(1)

    ring_end(wa.at[2], 2)
    invert(2)
    zq[2, NEAR, 0:32] = solve(wc[NEAR, 2, z, y])
    shift(has_near[2], zq.at[2, NEAR, pl.ds(0, 32)], rq.at[2, FAR, NEAR, pl.ds(0, 32)], ("q", 2, FAR), near[2])
    zq[2, FAR, 0:32] = solve(wc[FAR, 2, z, y])
    shift(has_far[2], zq.at[2, FAR, pl.ds(0, 32)], rq.at[2, NEAR, FAR, pl.ds(0, 32)], ("q", 2, NEAR), far[2])
    ring_relay(wc.at[NEAR, 2], 2, NEAR)
    ring_relay(wc.at[FAR, 2], 2, FAR)
    always = mirror >= 0
    pieces = 8
    ahead = 4
    step = source.shape[0] // pieces

    def piece(c):
        return pl.ds(step * c, step)

    def send_piece(c):
        if c % (pieces // 2) == 0:
            h = c // (pieces // 2)
            here = halves(h)
            shifted(has_near[1], rb.at[1, NEAR, here], ("b", 1, NEAR, h))
            shifted(has_far[1], rb.at[1, FAR, here], ("b", 1, FAR, h))
            source[here] = source[here] - couple(rb[1, NEAR, here], NEAR) - couple(rb[1, FAR, here], FAR)
            zb[2, here] = solve(source[here])
        shift(always, zb.at[2, piece(c)], rb.at[2, 0, piece(c)], ("c", c), mirror)

    for c in range(ahead):
        send_piece(c)
    for c in range(pieces):
        arrived(rb.at[2, 0, piece(c)], ("c", c))
        shift(has_onward, rb.at[2, 0, piece(c)], rb.at[2, 1, piece(c)], ("d", c), onward)
        if c + ahead < pieces:
            send_piece(c + ahead)
    ring_end(wc.at[NEAR, 2], 2, NEAR)
    hold(2, NEAR)
    ring_end(wc.at[FAR, 2], 2, FAR)
    hold(2, FAR)
    shifted(has_near[2], rq.at[2, NEAR, FAR, pl.ds(0, 32)], ("q", 2, NEAR))
    shifted(has_far[2], rq.at[2, FAR, NEAR, pl.ds(0, 32)], ("q", 2, FAR))
    a_out[...] = wa[2, z, y] - couple(rq[2, NEAR, FAR, 0:32], NEAR) - couple(rq[2, FAR, NEAR, 0:32], FAR)
    direct = (1 - toward * side) // 2
    source[...] = source[...] - couple(rb[2, 0], direct)
    for c in range(pieces):
        shifted(has_backward, rb.at[2, 1, piece(c)], ("d", c))
        if (c + 1) % (pieces // 2) == 0:
            here = halves(c // (pieces // 2))
            source[here] = source[here] - couple(rb[2, 1, here], 1 - direct)
    b_out[...] = source[...].T

    for there, out in sent:
        if there is None:
            out.wait_send()
        else:
            pl.when(there)(out.wait_send)


def shards(sectors, diag_blocks, lower_blocks, upper_blocks, sources):
    m = diag_blocks.shape[1]
    width = diag_blocks.shape[2]
    columns = sources.shape[2]
    quarter = m // 4
    copies = 128
    vmem = pl.BlockSpec(memory_space=pltpu.VMEM)
    hbm = pl.BlockSpec(memory_space=pl.ANY)
    center, source = pl.pallas_call(
        functools.partial(kernel, sectors, m),
        out_shape=(jax.ShapeDtypeStruct((width, m), F32), jax.ShapeDtypeStruct((m, columns), F32)),
        in_specs=[hbm] * 4,
        out_specs=(vmem, vmem),
        scratch_shapes=[
            pltpu.VMEM((LEVELS, 4, 4, width, m), F32),
            pltpu.VMEM((2, LEVELS, 4, 4, width, m), F32),
            pltpu.VMEM((LEVELS, 2, quarter, m), F32),
            pltpu.VMEM((m, m), F32),
            pltpu.VMEM((m, m), F32),
            pltpu.VMEM((LEVELS, 2, 2, quarter, m), F32),
            pltpu.VMEM((LEVELS, columns, m), F32),
            pltpu.VMEM((LEVELS, 2, columns, m), F32),
            pltpu.VMEM((m, columns), F32),
            pltpu.VMEM((columns, m), F32),
            pltpu.VMEM((m, m), BF16),
            pltpu.VMEM((m, m), BF16),
            pltpu.VMEM((2, m, m), BF16),
            pltpu.VMEM((2, m, m), BF16),
            pltpu.SemaphoreType.DMA((4,)),
            pltpu.SemaphoreType.DMA((copies,)),
            pltpu.SemaphoreType.DMA((copies,)),
        ],
        compiler_params=pltpu.CompilerParams(
            collective_id=0, has_side_effects=True, vmem_limit_bytes=56 * 2**20),
        name="reduction",
    )(diag_blocks[0].T, lower_blocks[0].T, upper_blocks[0].T, sources[0])
    return center.T[None], source[None]


def solution(mesh):
    placed = P("sec", None, "ch")
    return jax.shard_map(
        functools.partial(shards, mesh.shape["sec"]),
        mesh=mesh,
        in_specs=(placed,) * 4,
        out_specs=(placed, placed),
        check_vma=False,
    )
```

```python
import functools

import jax
import jax.numpy as jnp
from jax import lax
from jax.experimental import pallas as pl
from jax.experimental.pallas import tpu as pltpu
from jax.sharding import PartitionSpec as P

LEVELS = 3
NEAR, FAR = 0, 1
MESH = pl.DeviceIdType.MESH
F32 = jnp.float32
BF16 = jnp.bfloat16


def split(x):
    hi = x.astype(BF16)
    return hi, (x - hi.astype(F32)).astype(BF16)


def dot(a, b):
    return jnp.dot(a, b, preferred_element_type=F32)


def product(left, hi, lo):
    left_hi, left_lo = split(left)
    count = left.shape[0]
    both = dot(jnp.concatenate([left_hi, left_lo], axis=0), hi)
    return both[:count] + (both[count:] + dot(left_hi, lo))


class Slots:
    def __init__(self):
        self.taken = {}

    def __call__(self, *name):
        return self.taken.setdefault(name, len(self.taken))


def kernel(sectors, m, a_in, l_in, u_in, b_in, a_out, b_out,
           wa, wc, zq, zwhole, rwhole, rq, zb, rb, b_raw, source,
           inv_hi, inv_lo, c_hi, c_lo, load_sem, ssem, rsem):
    sec = lax.axis_index("sec")
    ch = lax.axis_index("ch")
    z, y = ch // 4, ch % 4
    core = sec % 2
    toward = 1 - 2 * core
    side = 1 - 2 * ((sec % 8) // 4)
    quarter = m // 4
    half_rows = source.shape[0] // 2

    loads = [
        pltpu.make_async_copy(a_in, wa.at[0, z, y], load_sem.at[0]),
        pltpu.make_async_copy(l_in, wc.at[1 - core, 0, z, y], load_sem.at[1]),
        pltpu.make_async_copy(u_in, wc.at[core, 0, z, y], load_sem.at[2]),
        pltpu.make_async_copy(b_in, b_raw, load_sem.at[3]),
    ]
    for load in loads:
        load.start()

    def zat(d):
        return (z + d) % 4

    def yat(d):
        return (y + d) % 4

    def inside(index):
        return jnp.logical_and(index >= 0, index < sectors)

    z_next, z_prev = (sec, zat(1) * 4 + y), (sec, zat(3) * 4 + y)
    y_next, y_prev, y_far = (sec, z * 4 + yat(1)), (sec, z * 4 + yat(3)), (sec, z * 4 + yat(2))
    near = [sec + toward * 2 ** k for k in range(LEVELS)]
    far = [sec - toward * 2 ** k for k in range(LEVELS)]
    has_near = [inside(i) for i in near]
    has_far = [inside(i) for i in far]
    mirror, onward, backward = sec + 4 * side, sec + 8 * side, sec - 8 * side
    has_onward, has_backward = inside(onward), inside(backward)

    barrier = pltpu.get_barrier_semaphore()

    def greet(device):
        pl.semaphore_signal(barrier, inc=1, device_id=device, device_id_type=MESH)

    for device in (z_next, z_prev, y_next, y_prev, y_far):
        greet(device)
    peers = 5
    for index, there in zip(near + far + [onward, backward], has_near + has_far + [has_onward, has_backward]):
        @pl.when(there)
        def _():
            greet((index, ch))

        peers = peers + there.astype(jnp.int32)
    pl.semaphore_wait(barrier, peers)
    for load in loads:
        load.wait()

    slots = Slots()
    sent = []

    def copy(src, dst, index, device):
        return pltpu.make_async_remote_copy(
            src_ref=src, dst_ref=dst, send_sem=ssem.at[index], recv_sem=rsem.at[index],
            device_id=device, device_id_type=MESH)

    def push(ref, name, device):
        out = copy(ref, ref, slots(*name), device)
        out.start()
        sent.append((None, out))

    def arrived(ref, name):
        copy(ref, ref, slots(*name), y_next).wait_recv()

    def shift(there, src, dst, name, target):
        out = copy(src, dst, slots(*name), (target, ch))

        @pl.when(there)
        def _():
            out.start()

        sent.append((there, out))

    def shifted(there, ref, name):
        @pl.when(there)
        def _():
            arrived(ref, name)

    whole = (wa.at[0], wc.at[FAR, 0], wc.at[NEAR, 0])

    def slab(i, dz, dy):
        return whole[i].at[zat(dz), yat(dy)]

    def half(i, dz, part):
        return whole[i].at[zat(dz), y, pl.ds(16 * part, 16)]

    def z_own(i):
        push(slab(i, 0, 0), ("z", i, 1), z_next)
        push(slab(i, 0, 0), ("z", i, 3), z_prev)

    def y_send(i, r):
        push(slab(i, r, 0), ("y", i, r, 1), y_next)
        push(slab(i, r, 0), ("y", i, r, 3), y_prev)
        if r % 2 == 0:
            push(slab(i, r, 0), ("y", i, r, 2), y_far)

    def y_half(i, r, dy, part):
        return whole[i].at[zat(r), yat(dy), pl.ds(16 * part, 16)]

    def y_relay(i):
        for r in (3, 1):
            arrived(slab(i, r, 3), ("y", i, r, 1))
            push(y_half(i, r, 3, 0), ("yy", i, r, 1), y_next)
            arrived(slab(i, r, 1), ("y", i, r, 3))
            push(y_half(i, r, 1, 1), ("yy", i, r, 3), y_prev)

    def z_relay(i):
        arrived(slab(i, 3, 0), ("z", i, 1))
        push(half(i, 3, 0), ("zz", i, 1), z_next)
        arrived(slab(i, 1, 0), ("z", i, 3))
        push(half(i, 1, 1), ("zz", i, 3), z_prev)
        y_send(i, 3)
        y_send(i, 1)

    def z_last(i):
        arrived(half(i, 2, 0), ("zz", i, 1))
        arrived(half(i, 2, 1), ("zz", i, 3))
        y_send(i, 2)

    seen = set()

    def y_wait(i, r):
        if (i, r) not in seen:
            seen.add((i, r))
            arrived(slab(i, r, 3), ("y", i, r, 1))
            arrived(slab(i, r, 1), ("y", i, r, 3))

    def y_last(i):
        for r in (0, 2):
            y_wait(i, r)
            arrived(slab(i, r, 2), ("y", i, r, 2))
        for r in (1, 3):
            arrived(y_half(i, r, 2, 0), ("yy", i, r, 1))
            arrived(y_half(i, r, 2, 1), ("yy", i, r, 3))

    def part(ref, dy, p):
        return ref.at[pl.ds(2 * p, 2), yat(dy)]

    def ring_start(ref, *tag):
        push(part(ref, 0, 0), ("r", *tag, 0), y_next)
        push(part(ref, 0, 1), ("r", *tag, 1), y_prev)
        push(part(ref, 0, 1), ("r", *tag, 2), y_next)
        push(part(ref, 0, 0), ("r", *tag, 3), y_prev)

    def ring_relay(ref, *tag):
        arrived(part(ref, 3, 0), ("r", *tag, 0))
        push(part(ref, 3, 0), ("r", *tag, 4), y_next)
        arrived(part(ref, 1, 1), ("r", *tag, 1))
        push(part(ref, 1, 1), ("r", *tag, 5), y_prev)

    def ring_end(ref, *tag):
        arrived(part(ref, 3, 1), ("r", *tag, 2))
        arrived(part(ref, 1, 0), ("r", *tag, 3))
        arrived(part(ref, 2, 0), ("r", *tag, 4))
        arrived(part(ref, 2, 1), ("r", *tag, 5))

    def rows(ref):
        return ref[...].reshape(m, m)

    def own(ref):
        return ref[:, y].reshape(quarter, m)

    def put(ref, value):
        ref[:, y] = value.reshape(4, quarter // 4, m)

    def invert(k):
        block = rows(wa.at[k])
        on = lax.broadcasted_iota(jnp.int32, (m, m), 0) == lax.broadcasted_iota(jnp.int32, (m, m), 1)
        diag = jnp.where(on, block, 0.0)
        across = 1.0 / jnp.sum(diag, axis=0, keepdims=True)
        down = 1.0 / jnp.sum(diag, axis=1, keepdims=True)
        start = jnp.where(on, across, -(down * block * across))
        block_hi, block_lo = split(block)
        start_hi, start_lo = split(start)
        inner = product(start, block_hi, block_lo)
        inv_hi[...], inv_lo[...] = split(2.0 * start - product(inner, start_hi, start_lo))

    def solve(value):
        return product(value, inv_hi[...], inv_lo[...])

    def couple(value, role):
        return product(value, c_hi[role], c_lo[role])

    def hold(k, role):
        c_hi[role], c_lo[role] = split(rows(wc.at[role, k]))

    z_own(0)
    y_send(0, 0)
    y_send(1, 0)
    y_send(2, 0)
    source[...] = b_raw[...].T

    def clear(there, ref):
        @pl.when(jnp.logical_not(there))
        def _():
            ref[...] = jnp.zeros_like(ref)

    clear(has_far[0], rq.at[0, FAR])
    clear(has_far[0], rb.at[0, FAR])
    for k in range(1, LEVELS):
        clear(has_near[k], rq.at[k, NEAR])
        clear(has_far[k], rq.at[k, FAR])
    clear(has_near[1], rb.at[1, NEAR])
    clear(has_far[1], rb.at[1, FAR])
    clear(has_backward, rb.at[2, 1])
    y_wait(0, 0)
    z_own(1)
    z_relay(0)
    z_own(2)
    y_relay(0)
    z_relay(1)
    y_relay(1)
    z_last(0)
    z_relay(2)
    y_last(0)
    invert(0)
    z_last(1)
    y_relay(2)
    z_last(2)

    zq[0, FAR] = solve(own(wc.at[FAR, 0]))
    shift(has_far[0], zq.at[0, FAR], rq.at[0, FAR, FAR], ("q", 0, FAR, FAR), far[0])
    zq[0, NEAR] = solve(own(wc.at[NEAR, 0]))
    shift(has_near[0], zq.at[0, NEAR], rq.at[0, NEAR, NEAR], ("q", 0, NEAR, NEAR), near[0])
    zb[0] = solve(source[...])
    y_last(1)
    hold(0, FAR)
    shifted(has_far[0], rq.at[0, FAR, FAR], ("q", 0, FAR, FAR))
    shift(has_far[0], zq.at[0, NEAR], rq.at[0, FAR, NEAR], ("q", 0, FAR, NEAR), far[0])
    center = own(wa.at[0]) - couple(rq[0, FAR, FAR], FAR)
    y_last(2)
    hold(0, NEAR)
    shifted(has_near[0], rq.at[0, NEAR, NEAR], ("q", 0, NEAR, NEAR))
    put(wa.at[1], center - couple(rq[0, NEAR, NEAR], NEAR))
    ring_start(wa.at[1], 1)
    shift(has_far[0], zb.at[0], rb.at[0, FAR], ("b", 0, FAR), far[0])
    shift(has_near[0], zb.at[0], rb.at[0, NEAR], ("b", 0, NEAR), near[0])
    zwhole[...] = solve(rows(wc.at[FAR, 0]))
    shift(has_near[0], zwhole, rwhole, ("w",), near[0])
    shifted(has_far[0], rq.at[0, FAR, NEAR], ("q", 0, FAR, NEAR))
    put(wc.at[FAR, 1], -couple(rq[0, FAR, NEAR], FAR))
    ring_relay(wa.at[1], 1)
    ring_start(wc.at[FAR, 1], 1, FAR)
    shifted(has_near[0], rwhole, ("w",))
    wc[NEAR, 1] = (-couple(rwhole[...], NEAR)).reshape(4, 4, quarter // 4, m)
    shifted(has_near[0], rb.at[0, NEAR], ("b", 0, NEAR))
    shifted(has_far[0], rb.at[0, FAR], ("b", 0, FAR))
    source[...] = source[...] - couple(rb[0, NEAR], NEAR) - couple(rb[0, FAR], FAR)

    def halves(h):
        return pl.ds(half_rows * h, half_rows)

    def send_half(h):
        shift(has_near[1], zb.at[1, halves(h)], rb.at[1, FAR, halves(h)], ("b", 1, FAR, h), near[1])
        shift(has_far[1], zb.at[1, halves(h)], rb.at[1, NEAR, halves(h)], ("b", 1, NEAR, h), far[1])

    ring_end(wa.at[1], 1)
    ring_relay(wc.at[FAR, 1], 1, FAR)
    invert(1)
    zq[1, NEAR] = solve(own(wc.at[NEAR, 1]))
    shift(has_near[1], zq.at[1, NEAR], rq.at[1, FAR, NEAR], ("q", 1, FAR, NEAR), near[1])
    zq[1, FAR] = solve(own(wc.at[FAR, 1]))
    shift(has_far[1], zq.at[1, FAR], rq.at[1, NEAR, FAR], ("q", 1, NEAR, FAR), far[1])
    zb[1] = solve(source[...])
    hold(1, NEAR)
    ring_end(wc.at[FAR, 1], 1, FAR)
    hold(1, FAR)
    shifted(has_near[1], rq.at[1, NEAR, FAR], ("q", 1, NEAR, FAR))
    shifted(has_far[1], rq.at[1, FAR, NEAR], ("q", 1, FAR, NEAR))
    shift(has_near[1], zq.at[1, FAR], rq.at[1, FAR, FAR], ("q", 1, FAR, FAR), near[1])
    shift(has_far[1], zq.at[1, NEAR], rq.at[1, NEAR, NEAR], ("q", 1, NEAR, NEAR), far[1])
    put(wa.at[2], own(wa.at[1]) - couple(rq[1, NEAR, FAR], NEAR) - couple(rq[1, FAR, NEAR], FAR))
    ring_start(wa.at[2], 2)
    ring_relay(wa.at[2], 2)
    send_half(0)
    shifted(has_near[1], rq.at[1, NEAR, NEAR], ("q", 1, NEAR, NEAR))
    put(wc.at[NEAR, 2], -couple(rq[1, NEAR, NEAR], NEAR))
    ring_start(wc.at[NEAR, 2], 2, NEAR)
    shifted(has_far[1], rq.at[1, FAR, FAR], ("q", 1, FAR, FAR))
    put(wc.at[FAR, 2], -couple(rq[1, FAR, FAR], FAR))
    ring_start(wc.at[FAR, 2], 2, FAR)
    send_half(1)

    ring_end(wa.at[2], 2)
    invert(2)
    zq[2, NEAR, 0:32] = solve(wc[NEAR, 2, z, y])
    shift(has_near[2], zq.at[2, NEAR, pl.ds(0, 32)], rq.at[2, FAR, NEAR, pl.ds(0, 32)], ("q", 2, FAR), near[2])
    zq[2, FAR, 0:32] = solve(wc[FAR, 2, z, y])
    shift(has_far[2], zq.at[2, FAR, pl.ds(0, 32)], rq.at[2, NEAR, FAR, pl.ds(0, 32)], ("q", 2, NEAR), far[2])
    ring_relay(wc.at[NEAR, 2], 2, NEAR)
    ring_relay(wc.at[FAR, 2], 2, FAR)
    always = mirror >= 0
    pieces = 8
    ahead = 4
    step = source.shape[0] // pieces

    def piece(c):
        return pl.ds(step * c, step)

    def send_piece(c):
        if c % (pieces // 2) == 0:
            h = c // (pieces // 2)
            here = halves(h)
            shifted(has_near[1], rb.at[1, NEAR, here], ("b", 1, NEAR, h))
            shifted(has_far[1], rb.at[1, FAR, here], ("b", 1, FAR, h))
            source[here] = source[here] - couple(rb[1, NEAR, here], NEAR) - couple(rb[1, FAR, here], FAR)
            zb[2, here] = solve(source[here])
        shift(always, zb.at[2, piece(c)], rb.at[2, 0, piece(c)], ("c", c), mirror)

    for c in range(ahead):
        send_piece(c)
    for c in range(pieces):
        arrived(rb.at[2, 0, piece(c)], ("c", c))
        shift(has_onward, rb.at[2, 0, piece(c)], rb.at[2, 1, piece(c)], ("d", c), onward)
        if c + ahead < pieces:
            send_piece(c + ahead)
    ring_end(wc.at[NEAR, 2], 2, NEAR)
    hold(2, NEAR)
    ring_end(wc.at[FAR, 2], 2, FAR)
    hold(2, FAR)
    shifted(has_near[2], rq.at[2, NEAR, FAR, pl.ds(0, 32)], ("q", 2, NEAR))
    shifted(has_far[2], rq.at[2, FAR, NEAR, pl.ds(0, 32)], ("q", 2, FAR))
    a_out[...] = wa[2, z, y] - couple(rq[2, NEAR, FAR, 0:32], NEAR) - couple(rq[2, FAR, NEAR, 0:32], FAR)
    direct = (1 - toward * side) // 2
    source[...] = source[...] - couple(rb[2, 0], direct)
    for c in range(pieces):
        shifted(has_backward, rb.at[2, 1, piece(c)], ("d", c))
        if (c + 1) % (pieces // 2) == 0:
            here = halves(c // (pieces // 2))
            source[here] = source[here] - couple(rb[2, 1, here], 1 - direct)
    b_out[...] = source[...].T

    for there, out in sent:
        if there is None:
            out.wait_send()
        else:
            pl.when(there)(out.wait_send)


def shards(sectors, diag_blocks, lower_blocks, upper_blocks, sources):
    m = diag_blocks.shape[1]
    width = diag_blocks.shape[2]
    columns = sources.shape[2]
    quarter = m // 4
    copies = 128
    vmem = pl.BlockSpec(memory_space=pltpu.VMEM)
    hbm = pl.BlockSpec(memory_space=pl.ANY)
    center, source = pl.pallas_call(
        functools.partial(kernel, sectors, m),
        out_shape=(jax.ShapeDtypeStruct((width, m), F32), jax.ShapeDtypeStruct((m, columns), F32)),
        in_specs=[hbm] * 4,
        out_specs=(vmem, vmem),
        scratch_shapes=[
            pltpu.VMEM((LEVELS, 4, 4, width, m), F32),
            pltpu.VMEM((2, LEVELS, 4, 4, width, m), F32),
            pltpu.VMEM((LEVELS, 2, quarter, m), F32),
            pltpu.VMEM((m, m), F32),
            pltpu.VMEM((m, m), F32),
            pltpu.VMEM((LEVELS, 2, 2, quarter, m), F32),
            pltpu.VMEM((LEVELS, columns, m), F32),
            pltpu.VMEM((LEVELS, 2, columns, m), F32),
            pltpu.VMEM((m, columns), F32),
            pltpu.VMEM((columns, m), F32),
            pltpu.VMEM((m, m), BF16),
            pltpu.VMEM((m, m), BF16),
            pltpu.VMEM((2, m, m), BF16),
            pltpu.VMEM((2, m, m), BF16),
            pltpu.SemaphoreType.DMA((4,)),
            pltpu.SemaphoreType.DMA((copies,)),
            pltpu.SemaphoreType.DMA((copies,)),
        ],
        compiler_params=pltpu.CompilerParams(
            collective_id=0, has_side_effects=True, vmem_limit_bytes=56 * 2**20),
        name="reduction",
    )(diag_blocks[0].T, lower_blocks[0].T, upper_blocks[0].T, sources[0])
    return center.T[None], source[None]


def solution(mesh):
    placed = P("sec", None, "ch")
    return jax.shard_map(
        functools.partial(shards, mesh.shape["sec"]),
        mesh=mesh,
        in_specs=(placed,) * 4,
        out_specs=(placed, placed),
        check_vma=False,
    )
```
